32 devices in a mesh: fsdp: 8 (over z, x), ctx: 4 (over y, core).
Axes of the slice: x: 2, y: 2, z: 4, core: 2. Of those that a mesh axis runs over, the one named last changes fastest.
Arguments:
- loaded: bfloat16 [8192, 12288], P(('fsdp', 'ctx')), may hold values from -6 to 6
- route: int32 [32, 8], P(('fsdp', 'ctx')), may hold values from 0 to 7, each once within a row
- doc_ids: int32 [8, 1024], P('fsdp'), may hold values from 0 to 7, never falling along the last dimension, each value on 1 to 512 neighbouring positions
- short_filter: float32 [7, 768], replicated, may hold values from -2 to 2
- medium_filter: bfloat16 [128, 256], replicated, may hold values from -0.5 to 0.5
- out_weight: bfloat16 [4096, 8192], P('fsdp', 'ctx'), may hold values from -0.09375 to 0.09375
Outputs:
- mixed: bfloat16 [8192, 8192], P(('fsdp', 'ctx'))
The draws below stay inside these ranges and needn't reach their ends.
Inputs may be any that keep to these rules, and one draw needn't show every extreme that they name: Each row of route names every sequence 0 to 7 exactly once. `doc_ids`: along each sequence the document numbers never fall; each document spans 1 to 512 positions and one spans exactly 512.
All inputs are finite; a program needn't handle non-finite values.
Results may differ from the reference program's by a relative error of at most 0.0058.
Values may be sent and summed in bfloat16 or wider, within the bound.
No kernel may reach another device: no remote copies, remote signals or barrier semaphores. Data moves between devices by JAX's collectives and lax.ppermute only.
A program may use at most 128 MiB of HBM per device.

```python
import math
import jax
import jax.numpy as jnp
import numpy as np
from jax import lax

D = 8192
CH = 4096
GSIZE = 16
KS = 7
KM = 128
DOCS = 8
LEN = 1024
TOKENS = 8192
BLK = 32
SGROUPS = 768
MGROUPS = 256
DOC_MOST = 512
N_FSDP = 8
N_CTX = 4


def block_levels(rng, shape, pieces, low, largest):
    def one(position, shards_of):
        heights = jax.random.uniform(jax.random.fold_in(jax.random.fold_in(rng, 6), position), (shards_of,), jnp.float32, low / len(pieces), largest / len(pieces))
        return jnp.repeat(jnp.exp(heights), shape[position] // shards_of).reshape((-1,) + (1,) * (len(shape) - position - 1))

    gain = one(*pieces[0])
    for cut in pieces[1:]:
        gain = gain * one(*cut)
    return gain


def length_profile(amount, total, reach, lean):
    weights = [(1 << 20) // math.isqrt(rank ** lean) + 1 for rank in range(2, amount + 1)]
    rest, holding = total - reach - (amount - 1), [1] * (amount - 1)
    while rest > 0:
        free = [i for i in range(amount - 1) if holding[i] < reach]
        whole, budget = sum([weights[i] for i in free]), rest
        for i in free:
            extra = min(reach - holding[i], max(1, budget * weights[i] // whole), rest)
            holding[i] = holding[i] + extra
            rest = rest - extra
    return np.array([reach] + holding)


def uneven_parts(rng, number_of, total, most, slope):
    if number_of == 2:
        one = jax.random.randint(rng, (), max(1, total - most), min(most, total - 1) + 1)
        return jnp.stack([one, total - one])
    tallies = jnp.asarray(length_profile(number_of, total, most, slope), jnp.int32)
    twos = (number_of - 1) // 2
    source_of, taker = tallies[1:1 + 2 * twos:2], tallies[2:2 + 2 * twos:2]
    margin = jnp.minimum(source_of - 1, most - taker)
    moved = jax.random.randint(jax.random.fold_in(rng, 1), (twos,), 0, 1 << 20) % (margin + 1)
    tallies = tallies.at[1:1 + 2 * twos:2].set(source_of - moved).at[2:2 + 2 * twos:2].set(taker + moved)
    return tallies[jax.random.permutation(jax.random.fold_in(rng, 2), number_of)]


def gaussian(stream_key, dims, width, most, split=(), held_as=jnp.bfloat16):
    entries = jax.random.normal(stream_key, dims, jnp.float32) * width
    if len(split) > 0:
        entries = block_levels(stream_key, dims, split, -0.22, 0.18) * entries
    return jnp.clip(entries, min=-most, max=most).astype(held_as)


def setup_inputs(seed: int = 0) -> dict:
    key_of = jax.random.split(jax.random.key(seed), 7)
    return {
        "loaded": gaussian(key_of[0], (TOKENS, 3 * CH), 1.0, 6.0, ((0, 32),)),
        "route": jax.vmap(lambda own: jax.random.permutation(own, N_FSDP))(jax.random.split(key_of[1], (N_FSDP * N_CTX))).reshape((N_FSDP * N_CTX, N_FSDP)).astype(jnp.int32),
        "doc_ids": jax.vmap(lambda own: jnp.searchsorted(jnp.cumsum(uneven_parts(own, DOCS, LEN, DOC_MOST, 2)), jnp.arange(LEN), side="right"))(jax.random.split(key_of[2], N_FSDP)).reshape((N_FSDP, LEN)).astype(jnp.int32),
        "short_filter": gaussian(key_of[3], (KS, SGROUPS), KS ** -0.5, 2.0, (), jnp.float32),
        "medium_filter": gaussian(key_of[4], (KM, MGROUPS), KM ** -0.5, 0.5),
        "out_weight": gaussian(key_of[5], (CH, D), CH ** -0.5, 0.09375, ((0, 8), (1, 4))),
    }


def reference(loaded, route, doc_ids, short_filter, medium_filter, out_weight):
    blocks = loaded.reshape(N_FSDP, N_CTX, N_FSDP, BLK, 3 * CH)
    inverse = jnp.argsort(route.reshape(N_FSDP, N_CTX, N_FSDP), axis=-1).astype(jnp.int32)
    short_full = jnp.repeat(short_filter.astype(jnp.float32), GSIZE, axis=1)
    medium_full = jnp.repeat(medium_filter.astype(jnp.float32), GSIZE, axis=1)
    loader_rows = jnp.arange(N_FSDP, dtype=jnp.int32)[:, None]
    context_cols = jnp.arange(N_CTX, dtype=jnp.int32)[None, :]

    def one_sequence(owner_row):
        picked = inverse[:, :, owner_row]
        gathered = blocks[loader_rows, context_cols, picked]
        features = jnp.transpose(gathered, (1, 0, 2, 3)).reshape(LEN, 3 * CH).astype(jnp.float32)
        doc_rows = doc_ids[owner_row]
        short_pad = jnp.concatenate([jnp.zeros((KS - 1, 3 * CH), jnp.float32), features], axis=0)
        short_ids = jnp.concatenate([jnp.full((KS - 1,), -1, jnp.int32), doc_rows], axis=0)
        summed = jnp.zeros((LEN, 3 * CH), jnp.float32)
        for offset in range(KS):
            shifted = short_pad[KS - 1 - offset: KS - 1 - offset + LEN]
            same_doc = (short_ids[KS - 1 - offset: KS - 1 - offset + LEN] == doc_rows).astype(jnp.float32)[:, None]
            summed = summed + short_full[offset][None, :] * shifted * same_doc
        query = summed[:, :CH]
        gate_in = (summed[:, CH:2 * CH] * summed[:, 2 * CH:]).astype(jnp.bfloat16)
        gate_pad = jnp.concatenate([jnp.zeros((KM - 1, CH), jnp.float32), gate_in.astype(jnp.float32)], axis=0)
        gate_ids = jnp.concatenate([jnp.full((KM - 1,), -1, jnp.int32), doc_rows], axis=0)

        def add_offset(offset, running):
            first_row = (KM - 1 - offset).astype(jnp.int32)
            shifted = lax.dynamic_slice_in_dim(gate_pad, first_row, LEN, 0)
            shift_ids = lax.dynamic_slice_in_dim(gate_ids, first_row, LEN, 0)
            same_doc = (shift_ids == doc_rows).astype(jnp.float32)[:, None]
            filter_tap = lax.dynamic_slice_in_dim(medium_full, offset.astype(jnp.int32), 1, 0)
            return running + filter_tap * shifted * same_doc

        medium = lax.fori_loop(0, KM, add_offset, jnp.zeros((LEN, CH), jnp.float32))
        gated = (query * medium).astype(jnp.bfloat16)
        return jnp.dot(gated, out_weight, preferred_element_type=jnp.float32).astype(jnp.bfloat16)

    outputs = lax.map(one_sequence, jnp.arange(N_FSDP, dtype=jnp.int32))
    return outputs.reshape(TOKENS, D)
```

```python
import functools

import jax
import jax.numpy as jnp
from jax import lax
from jax.experimental import pallas as pl
from jax.experimental.pallas import tpu as pltpu
from jax.sharding import Mesh
from jax.sharding import PartitionSpec as P

FSDP = ("fh", "fx")
CTX = ("y", "core")
PLANE = ("fx", "y", "core")
EVERY = ("fh", "fx", "y", "core")
SWAP = [(0, 1), (1, 0)]
CHUNKS = 4
PANELS = 2
ROWS = 128
LANES = 128
MIB = 1 << 20


def short_kernel(order, q, k, v, hq, hk, hv, fq, fk, fv, mask, out, ext):
    rows, wide = q.shape[1], q.shape[2]
    taps = hq.shape[1] + 1
    pad = 8
    part = min(256, wide)
    for first in range(0, wide, part):
        cols = slice(first, first + part)

        def conv(block, halo, taps_ref):
            ext[pad - (taps - 1) : pad] = halo[0, :, cols].astype(jnp.float32)
            ext[pad : pad + rows] = block[0, :, cols].astype(jnp.float32)
            total = None
            for i in range(taps):
                term = taps_ref[i : i + 1, cols] * ext[pad - i : pad - i + rows]
                term = term * mask[0, :, i : i + 1]
                total = term if total is None else total + term
            return total

        out[0, :, first : first + part] = conv(q, hq, fq).astype(jnp.bfloat16)
        gate = conv(k, hk, fk) * conv(v, hv, fv)
        out[0, :, wide + first : wide + first + part] = gate.astype(jnp.bfloat16)


def short_call(order, blocks, halo, taps_full, mask, chunk):
    count, rows, wide = blocks.shape
    cols = wide // 3 // CHUNKS

    def of_block(part):
        return pl.BlockSpec((1, rows, cols), lambda g, o: (o[g], 0, part * CHUNKS + chunk))

    def of_halo(part):
        return pl.BlockSpec((1, halo.shape[1], cols), lambda g, o: (g, 0, part))

    def of_taps(part):
        return pl.BlockSpec((taps_full.shape[0], cols), lambda g, o: (0, part * CHUNKS + chunk))

    parts = range(3)
    return pl.pallas_call(
        short_kernel,
        grid_spec=pltpu.PrefetchScalarGridSpec(
            num_scalar_prefetch=1,
            grid=(count,),
            in_specs=[of_block(p) for p in parts]
            + [of_halo(p) for p in parts]
            + [of_taps(p) for p in parts]
            + [pl.BlockSpec((1,) + mask.shape[1:], lambda g, o: (g, 0, 0))],
            out_specs=pl.BlockSpec((1, rows, 2 * cols), lambda g, o: (g, 0, 0)),
            scratch_shapes=[pltpu.VMEM((8 + rows, min(256, cols)), jnp.float32)],
        ),
        out_shape=jax.ShapeDtypeStruct((count, rows, 2 * cols), jnp.bfloat16),
        cost_estimate=pl.CostEstimate(
            flops=count * rows * cols * 64, bytes_accessed=count * rows * cols * 10, transcendentals=0
        ),
        name="short_conv",
    )(order, blocks, blocks, blocks, halo, halo, halo, taps_full, taps_full, taps_full, mask)


def medium_kernel(group_size, q, gate, halo, table, same, out):
    groups = table.shape[0]
    lane = lax.broadcasted_iota(jnp.int32, (ROWS, LANES), 1) // group_size
    for a in range(gate.shape[0] // ROWS):
        rows = slice(a * ROWS, (a + 1) * ROWS)
        before = halo[...] if a == 0 else gate[(a - 1) * ROWS : a * ROWS]
        window = jnp.concatenate([before, gate[rows]], axis=0)
        total = jnp.zeros((ROWS, LANES), jnp.float32)
        for n in range(groups):
            matrix = table[n] * same[a]
            result = jnp.dot(matrix, window, preferred_element_type=jnp.float32)
            total = jnp.where(lane == n, result, total)
        out[rows] = (q[rows].astype(jnp.float32) * total).astype(jnp.bfloat16)


def medium_call(routed, halo, table, same, chunk, group_size):
    rows, cols = routed.shape[0], routed.shape[1] // 2
    steps = cols // LANES
    groups = LANES // group_size
    return pl.pallas_call(
        functools.partial(medium_kernel, group_size),
        grid=(steps,),
        in_specs=[
            pl.BlockSpec((rows, LANES), lambda t: (0, t)),
            pl.BlockSpec((rows, LANES), lambda t: (0, steps + t)),
            pl.BlockSpec((ROWS, LANES), lambda t: (0, t)),
            pl.BlockSpec((groups, ROWS, 2 * ROWS), lambda t: (chunk * steps + t, 0, 0)),
            pl.BlockSpec(same.shape, lambda t: (0, 0, 0)),
        ],
        out_specs=pl.BlockSpec((rows, LANES), lambda t: (0, t)),
        out_shape=jax.ShapeDtypeStruct((rows, cols), jnp.bfloat16),
        cost_estimate=pl.CostEstimate(
            flops=rows * cols * 1024 * 4, bytes_accessed=rows * cols * 24, transcendentals=0
        ),
        name="medium_conv",
    )(routed, routed, halo, table, same)


def project_kernel(*refs):
    pieces, panel, out = refs[:-2], refs[-2], refs[-1]
    depth = pieces[0].shape[1]
    total = None
    for j, piece in enumerate(pieces):
        term = jnp.dot(
            piece[...], panel[j * depth : (j + 1) * depth], preferred_element_type=jnp.float32
        )
        total = term if total is None else total + term
    out[...] = total.astype(jnp.bfloat16)


def project_call(pieces, panel):
    rows, depth = pieces[0].shape
    cols = panel.shape[1]
    tile = 512
    return pl.pallas_call(
        project_kernel,
        grid=(rows // tile,),
        in_specs=[pl.BlockSpec((tile, depth), lambda m: (m, 0)) for _ in pieces]
        + [pl.BlockSpec(panel.shape, lambda m: (0, 0))],
        out_specs=pl.BlockSpec((tile, cols), lambda m: (m, 0)),
        out_shape=jax.ShapeDtypeStruct((rows, cols), jnp.bfloat16),
        compiler_params=pltpu.CompilerParams(vmem_limit_bytes=40 * MIB),
        cost_estimate=pl.CostEstimate(
            flops=2 * rows * cols * panel.shape[0],
            bytes_accessed=2 * (rows * panel.shape[0] + panel.size + rows * cols),
            transcendentals=0,
        ),
        name="project",
    )(*pieces, panel)


def plane_gather(value):
    stacked = value[None, None, None]
    for axis, name in enumerate(PLANE):
        other = lax.ppermute(stacked, name, SWAP)
        first = lax.axis_index(name) == 0
        stacked = jnp.concatenate(
            [jnp.where(first, stacked, other), jnp.where(first, other, stacked)], axis=axis
        )
    return stacked.reshape(-1, value.shape[1])


def toeplitz(medium_filter):
    taps, groups = medium_filter.shape
    u = jnp.arange(ROWS, dtype=jnp.int32)[:, None]
    s = jnp.arange(2 * ROWS, dtype=jnp.int32)[None, :]
    offset = (u + ROWS - s).reshape(-1)
    onehot = (jnp.arange(taps, dtype=jnp.int32)[:, None] == offset[None, :]).astype(jnp.bfloat16)
    table = lax.dot_general(
        medium_filter, onehot, (((0,), (0,)), ((), ())), preferred_element_type=jnp.float32
    )
    return table.astype(jnp.bfloat16).reshape(groups, ROWS, 2 * ROWS)


def on_device(loaded, route, doc_ids, short_filter, medium_filter, out_weight):
    tok_rows, wide = loaded.shape
    channels = wide // 3
    count = lax.axis_size(FSDP)
    ctx_count = lax.axis_size(CTX)
    blk = tok_rows // count
    short_len = short_filter.shape[0]
    depth = short_len - 1
    medium_len = medium_filter.shape[0]
    group_size = wide // short_filter.shape[1]
    length = doc_ids.shape[1]
    cols = channels // CHUNKS
    ctx_at = lax.axis_index(CTX)
    f_at = lax.axis_index(FSDP)
    x_at = lax.axis_index("fx")

    seqs = jnp.arange(count, dtype=jnp.int32)
    order = jnp.sum(jnp.where(route[0][None, :] == seqs[:, None], seqs[None, :], 0), axis=1)
    blocks = loaded.reshape(count, blk, wide)
    tails = jnp.take(blocks[:, blk - depth :], order, axis=0, mode="clip")
    tails = tails.reshape(count, depth, 3, CHUNKS, cols)
    shift = []
    for f in range(count):
        for c in range(ctx_count):
            if f + 1 < count:
                shift.append((f * ctx_count + c, (f + 1) * ctx_count + c))
            elif c + 1 < ctx_count:
                shift.append((f * ctx_count + c, c + 1))
    halos = []
    for j in range(CHUNKS):
        tail = tails[:, :, :, j].reshape(count * depth, 3 * cols)
        halos.append(lax.ppermute(tail, EVERY, shift).reshape(count, depth, 3 * cols))

    all_ids = lax.all_gather(doc_ids, FSDP, axis=0, tiled=True)
    padded = jnp.concatenate([jnp.full((count, depth), -1, jnp.int32), all_ids], axis=1)
    near = lax.dynamic_slice_in_dim(padded, ctx_at * tok_rows + f_at * blk, depth + blk, 1)
    mask = jnp.stack(
        [near[:, depth - i : depth - i + blk] == near[:, depth:] for i in range(short_len)], axis=-1
    ).astype(jnp.float32)
    taps_full = jnp.repeat(short_filter, group_size, axis=1)

    half = out_weight.shape[1] // 2
    keep = lax.dynamic_slice_in_dim(out_weight, x_at * half, half, 1)
    give = lax.dynamic_slice_in_dim(out_weight, (1 - x_at) * half, half, 1)
    got = lax.ppermute(give, "fx", SWAP)
    low = x_at == 0
    weight = jnp.concatenate([jnp.where(low, keep, got), jnp.where(low, got, keep)], axis=0)

    table = toeplitz(medium_filter)
    own = jnp.concatenate([jnp.full((ROWS,), -1, jnp.int32), doc_ids[0]])
    own = lax.dynamic_slice_in_dim(own, ctx_at * tok_rows, ROWS + tok_rows, 0)
    same = jnp.stack(
        [
            own[ROWS + a : 2 * ROWS + a][:, None] == own[a : 2 * ROWS + a][None, :]
            for a in range(0, tok_rows, ROWS)
        ]
    ).astype(jnp.bfloat16)

    next_ctx = [(c, c + 1) for c in range(ctx_count - 1)]
    pieces = []
    routed_all = []
    for j in range(CHUNKS):
        sent = short_call(order, blocks, halos[j], taps_full, mask, j)
        routed = lax.all_to_all(sent, FSDP, split_axis=0, concat_axis=0, tiled=True)
        routed = routed.reshape(tok_rows, 2 * cols)
        routed_all.append(routed)
        before = lax.ppermute(routed[tok_rows - ROWS :, cols:], CTX, next_ctx)
        gated = medium_call(routed, before, table, same, j, group_size)
        pieces.append(plane_gather(gated))

    ncols = half // PANELS
    outs = []
    for n in range(PANELS):
        panel = lax.all_gather(
            weight[:, n * ncols : (n + 1) * ncols], "fh", axis=0, tiled=True
        )
        product = project_call(pieces, panel)
        product = product.reshape(-1, tok_rows, ncols)
        outs.append(lax.all_to_all(product, PLANE, split_axis=0, concat_axis=0, tiled=True))
    full = jnp.stack(outs, axis=0).reshape(PANELS, 2, ctx_count, tok_rows, ncols)
    return full.transpose(3, 2, 1, 0, 4).reshape(tok_rows, -1)


def solution(mesh):
    count, ctx_count = mesh.devices.shape
    fine = Mesh(mesh.devices.reshape(count // 2, 2, ctx_count // 2, 2), EVERY)
    placed = (
        P(EVERY, None),
        P(EVERY, None),
        P(FSDP, None),
        P(),
        P(),
        P(FSDP, CTX),
    )
    return jax.shard_map(
        on_device, mesh=fine, in_specs=placed, out_specs=P(EVERY, None), check_vma=False
    )
```

```python
import functools

import jax
import jax.numpy as jnp
from jax import lax
from jax.experimental import pallas as pl
from jax.experimental.pallas import tpu as pltpu
from jax.sharding import Mesh
from jax.sharding import PartitionSpec as P

FSDP = ("fh", "fx")
CTX = ("y", "core")
PLANE = ("fx", "y", "core")
EVERY = ("fh", "fx", "y", "core")
SWAP = [(0, 1), (1, 0)]
CHUNKS = 4
QUARTERS = 4
PANEL_STEPS = (("keep", 0, 2, 1, 3), ("keep", 2, 2, 3, 5), ("got", 0, 2, 4, 6), ("got", 2, 2, 5, 9))
FENCED = 5
PROJECTS = ((0, 2), (2, 2))
ROWS = 128
LANES = 128
MIB = 1 << 20
LIGHT = pl.CostEstimate(flops=1, bytes_accessed=1, transcendentals=0)


def short_kernel(order, order_prev, q, k, v, hq, hk, hv, fq, fk, fv, mask, out, ext):
    rows, wide = q.shape[1], q.shape[2]
    taps = hq.shape[1] + 1
    pad = 8
    linked = [jnp.broadcast_to(mask[0, :, i : i + 1], (rows, LANES)) for i in range(1, taps)]
    for first in range(0, wide, LANES):
        cols = slice(first, first + LANES)

        def conv(slot, block, halo, taps_ref):
            ext[slot, pad - (taps - 1) : pad] = halo[0, :, cols].astype(jnp.float32)
            own = block[0, :, cols].astype(jnp.float32)
            ext[slot, pad : pad + rows] = own
            total = taps_ref[0:1, cols] * own
            for i in range(1, taps):
                near = ext[slot, pad - i : pad - i + rows] * linked[i - 1]
                total = total + taps_ref[i : i + 1, cols] * near
            return total

        out[0, :, first : first + LANES] = conv(0, q, hq, fq).astype(jnp.bfloat16)
        gate = conv(1, k, hk, fk) * conv(2, v, hv, fv)
        out[0, :, wide + first : wide + first + LANES] = gate.astype(jnp.bfloat16)


def short_call(order, order_prev, blocks, halo, taps_full, mask, chunk):
    count, rows, wide = blocks.shape
    cols = wide // 3 // CHUNKS

    def of_block(part):
        return pl.BlockSpec((1, rows, cols), lambda g, o, p: (o[g], 0, part * CHUNKS + chunk))

    def of_halo(part):
        return pl.BlockSpec((1, halo.shape[1], cols), lambda g, o, p: (p[g], 0, part * CHUNKS + chunk))

    def of_taps(part):
        return pl.BlockSpec((taps_full.shape[0], cols), lambda g, o, p: (0, part * CHUNKS + chunk))

    parts = range(3)
    return pl.pallas_call(
        short_kernel,
        grid_spec=pltpu.PrefetchScalarGridSpec(
            num_scalar_prefetch=2,
            grid=(count,),
            in_specs=[of_block(p) for p in parts]
            + [of_halo(p) for p in parts]
            + [of_taps(p) for p in parts]
            + [pl.BlockSpec((1,) + mask.shape[1:], lambda g, o, p: (g, 0, 0))],
            out_specs=pl.BlockSpec((1, rows, 2 * cols), lambda g, o, p: (g, 0, 0)),
            scratch_shapes=[pltpu.VMEM((3, 8 + rows, LANES), jnp.float32)],
        ),
        out_shape=jax.ShapeDtypeStruct((count, rows, 2 * cols), jnp.bfloat16),
        cost_estimate=LIGHT,
        name="short_conv",
    )(order, order_prev, blocks, blocks, blocks, halo, halo, halo, taps_full, taps_full, taps_full, mask)


def medium_kernel(group_size, q, gate, halo, taps, same, out):
    blocks = gate.shape[0] // ROWS
    lane = lax.broadcasted_iota(jnp.int32, (ROWS, LANES), 1) // group_size
    windows, totals = [], []
    for a in range(blocks):
        before = halo[...] if a == 0 else gate[(a - 1) * ROWS : a * ROWS]
        windows.append(jnp.concatenate([before, gate[a * ROWS : (a + 1) * ROWS]], axis=0))
        totals.append(jnp.zeros((ROWS, LANES), jnp.float32))
    for n in range(taps.shape[0]):
        row = jnp.broadcast_to(taps[n : n + 1], (ROWS, 2 * ROWS))
        matrix = pltpu.roll(row, 0, 1, stride=1, stride_axis=0).astype(jnp.bfloat16)
        for a in range(blocks):
            result = jnp.dot(matrix * same[a], windows[a], preferred_element_type=jnp.float32)
            totals[a] = jnp.where(lane == n, result, totals[a])
    for a in range(blocks):
        rows = slice(a * ROWS, (a + 1) * ROWS)
        out[rows] = (q[rows].astype(jnp.float32) * totals[a]).astype(jnp.bfloat16)


def medium_call(routed, halo, taps, same, chunk, group_size):
    rows, cols = routed.shape[0], routed.shape[1] // 2
    steps = cols // LANES
    groups = LANES // group_size
    return pl.pallas_call(
        functools.partial(medium_kernel, group_size),
        grid=(steps,),
        in_specs=[
            pl.BlockSpec((rows, LANES), lambda t: (0, t)),
            pl.BlockSpec((rows, LANES), lambda t: (0, steps + t)),
            pl.BlockSpec((ROWS, LANES), lambda t: (0, t)),
            pl.BlockSpec((groups, 2 * ROWS), lambda t: (chunk * steps + t, 0)),
            pl.BlockSpec(same.shape, lambda t: (0, 0, 0)),
        ],
        out_specs=pl.BlockSpec((rows, LANES), lambda t: (0, t)),
        out_shape=jax.ShapeDtypeStruct((rows, cols), jnp.bfloat16),
        cost_estimate=LIGHT,
        name="medium_conv",
    )(routed, routed, halo, taps, same)


def project_kernel(count, side, dest, *refs):
    pieces, panels, out = refs[:-3], refs[-3:-1], refs[-1]
    held, depth = pieces[0].shape
    tile = out.shape[0] // count
    for half in range(2):
        given = pieces[half * len(pieces) // 2 : (half + 1) * len(pieces) // 2]
        total = None
        for m, piece in enumerate(given):
            i, other = m // 2, m % 2
            rows = panels[other][i * depth : (i + 1) * depth]
            term = jnp.dot(piece[...], rows, preferred_element_type=jnp.float32)
            total = term if total is None else total + term
        total = total.astype(jnp.bfloat16)
        for m in range(held // tile):
            at = pl.multiple_of(dest[half * held // tile + m] * tile, tile)
            out[pl.ds(at, tile)] = total[m * tile : (m + 1) * tile]


def project_call(side, dest, here, there, panels, cols, depth):
    held, wide = here[0].shape
    tile = min(256, cols)

    def specs():
        for i in range(wide // (2 * depth)):
            for other in range(2):
                yield pl.BlockSpec(
                    (held, depth),
                    lambda n, s, d, i=i, other=other: (0, 2 * i + (s[0] + other) % 2),
                    pipeline_mode=pl.Buffered(1),
                )

    given = [x for x in list(here) + list(there) for _ in range(wide // depth)]
    return pl.pallas_call(
        functools.partial(project_kernel, dest.shape[0]),
        grid_spec=pltpu.PrefetchScalarGridSpec(
            num_scalar_prefetch=2,
            grid=(cols // tile,),
            in_specs=[spec for _ in list(here) + list(there) for spec in specs()]
            + [
                pl.BlockSpec((p.shape[0], tile), lambda n, s, d, at=at // tile: (0, at + n))
                for p, at in panels
            ],
            out_specs=pl.BlockSpec((2 * held, tile), lambda n, s, d: (0, n)),
        ),
        out_shape=jax.ShapeDtypeStruct((2 * held, cols), jnp.bfloat16),
        compiler_params=pltpu.CompilerParams(vmem_limit_bytes=56 * MIB),
        cost_estimate=LIGHT,
        name="project",
    )(side, dest, *given, *(p for p, _ in panels))


def stack_kernel(*refs):
    out = refs[-1]
    rows = refs[0].shape[0]
    for m, piece in enumerate(refs[:-1]):
        out[m * rows : (m + 1) * rows] = piece[...]


def stack_call(pieces):
    rows, cols = pieces[0].shape
    tile = min(256, cols)
    return pl.pallas_call(
        stack_kernel,
        grid=(cols // tile,),
        in_specs=[pl.BlockSpec((rows, tile), lambda n: (0, n)) for _ in pieces],
        out_specs=pl.BlockSpec((len(pieces) * rows, tile), lambda n: (0, n)),
        out_shape=jax.ShapeDtypeStruct((len(pieces) * rows, cols), pieces[0].dtype),
        cost_estimate=LIGHT,
        name="stack",
    )(*pieces)


def place_kernel(*refs):
    out, at = refs[-1], 0
    for part in refs[:-1]:
        out[:, at : at + part.shape[2]] = part[0]
        at += part.shape[2]


def place_call(parts, ctx_count):
    count, rows = parts[0].shape[:2]
    wide = sum(p.shape[2] for p in parts)
    return pl.pallas_call(
        place_kernel,
        grid=(count,),
        in_specs=[pl.BlockSpec((1, rows, p.shape[2]), lambda s: (s, 0, 0)) for p in parts],
        out_specs=pl.BlockSpec(
            (rows, wide), lambda s: (0, (s % ctx_count) * (count // ctx_count) + s // ctx_count)
        ),
        out_shape=jax.ShapeDtypeStruct((rows, count * wide), parts[0].dtype),
        compiler_params=pltpu.CompilerParams(vmem_limit_bytes=16 * MIB),
        cost_estimate=LIGHT,
        name="place",
    )(*parts)


def after(value, *others):
    return lax.optimization_barrier((value,) + others)[0]


def on_device(loaded, route, doc_ids, short_filter, medium_filter, out_weight):
    tok_rows, wide = loaded.shape
    channels = wide // 3
    count = lax.axis_size(FSDP)
    ctx_count = lax.axis_size(CTX)
    blk = tok_rows // count
    short_len = short_filter.shape[0]
    depth = short_len - 1
    medium_len = medium_filter.shape[0]
    group_size = wide // short_filter.shape[1]
    length = doc_ids.shape[1]
    cols = channels // CHUNKS
    ctx_at = lax.axis_index(CTX)
    f_at = lax.axis_index(FSDP)
    x_at = lax.axis_index("fx")

    shift = []
    for f in range(count):
        for c in range(ctx_count):
            if f + 1 < count:
                shift.append((f * ctx_count + c, (f + 1) * ctx_count + c))
            elif c + 1 < ctx_count:
                shift.append((f * ctx_count + c, c + 1))

    seqs = jnp.arange(count, dtype=jnp.int32)
    order = jnp.sum(jnp.where(route[0][None, :] == seqs[:, None], seqs[None, :], 0), axis=1)
    order_prev = lax.ppermute(order, EVERY, shift)
    blocks = loaded.reshape(count, blk, wide)
    tail = blocks[:, blk - depth :].reshape(count * depth, wide)
    halo = lax.ppermute(tail, EVERY, shift).reshape(count, depth, wide)
    own_ids = jnp.concatenate([jnp.full((depth,), -1, jnp.int32), doc_ids[0]])
    own_ids = lax.dynamic_slice_in_dim(own_ids, ctx_at * tok_rows, depth + tok_rows, 0)
    near = jnp.stack([own_ids[f * blk : (f + 1) * blk + depth] for f in range(count)])
    near = after(near, tail)
    near = lax.all_to_all(near, FSDP, split_axis=0, concat_axis=0, tiled=True)


    taps_full = jnp.repeat(short_filter, group_size, axis=1)

    half = out_weight.shape[1] // 2
    keep = lax.dynamic_slice_in_dim(out_weight, x_at * half, half, 1)
    give = lax.dynamic_slice_in_dim(out_weight, (1 - x_at) * half, half, 1)

    reach = ROWS - medium_len
    medium_rows = jnp.pad(
        medium_filter.astype(jnp.float32)[::-1].T, ((0, 0), (reach + 1, ROWS - 1))
    )
    own = jnp.concatenate([jnp.full((ROWS,), -1, jnp.int32), doc_ids[0]])
    own = lax.dynamic_slice_in_dim(own, ctx_at * tok_rows, ROWS + tok_rows, 0)
    same = jnp.stack(
        [
            own[ROWS + a : 2 * ROWS + a][:, None] == own[a : 2 * ROWS + a][None, :]
            for a in range(0, tok_rows, ROWS)
        ]
    ).astype(jnp.bfloat16)

    next_ctx = [(c, c + 1) for c in range(ctx_count - 1)]

    def exchange(sent):
        routed = lax.all_to_all(sent, FSDP, split_axis=0, concat_axis=0, tiled=True)
        return routed.reshape(tok_rows, 2 * cols)

    live, flying = {}, {}
    def cut_panels(kind, value):
        for k, first, wide, _, _ in PANEL_STEPS:
            if k == kind:
                at = half // QUARTERS * first
                live["part", kind, first] = value[:, at : at + half // QUARTERS * wide]

    cut_panels("keep", keep)

    def fence(step):
        for key in [k for k, (due, _) in flying.items() if due <= step]:
            live[key] = flying.pop(key)[1]
        if step > FENCED:
            return
        keys = list(live)
        for key, value in zip(keys, lax.optimization_barrier([live[k] for k in keys])):
            live[key] = value

    def start_panels(step):
        for kind, first, wide, begin, due in PANEL_STEPS:
            if begin == step:
                source = live.pop(("part", kind, first))
                flying[kind, first, wide] = (due, lax.all_gather(source, "fh", axis=0, tiled=True))

    start_panels(0)
    halo, near, order_prev = lax.optimization_barrier((halo, near, order_prev))
    mask = jnp.stack(
        [near[:, depth - i : depth - i + blk] == near[:, depth:] for i in range(short_len)], axis=-1
    ).astype(jnp.float32)
    live["give"] = give
    live["sent", 0] = short_call(order, order_prev, blocks, halo, taps_full, mask, 0)
    live["mask"] = mask
    live["prior"] = order_prev
    live["medium"] = medium_rows
    live["same"] = same
    last = CHUNKS + 4
    for step in range(1, last + 1):
        if "got" in live:
            cut_panels("got", live.pop("got"))
        fence(step)
        start_panels(step)
        if step == 1:
            flying["got"] = (3, lax.ppermute(live.pop("give"), "fx", SWAP))
        if step <= CHUNKS:
            flying["routed", step - 1] = (step, exchange(live.pop(("sent", step - 1))))
        j = step - 5
        if 0 <= j < CHUNKS:
            here = stack_call([live.pop((k, j)) for k in ("gated", "by_y", "by_x", "by_both")])
            flying["here", j] = (step, here)
            flying["there", j] = (step + 1, lax.ppermute(here, "core", SWAP))
        j = step - 4
        if 0 <= j < CHUNKS:
            flying["by_both", j] = (step, lax.ppermute(live["by_x", j], "y", SWAP))
        j = step - 3
        if 0 <= j < CHUNKS:
            flying["by_x", j] = (step, lax.ppermute(live["gated", j], "fx", SWAP))
            flying["by_y", j] = (step, lax.ppermute(live["gated", j], "y", SWAP))
        j = step - 2
        if 0 <= j < CHUNKS:
            routed = live.pop(("routed", j))
            before = lax.ppermute(routed[tok_rows - ROWS :, cols:], CTX, next_ctx)
            gated = medium_call(routed, before, live["medium"], live["same"], j, group_size)
            flying["gated", j] = (step, gated)
        if step < CHUNKS:
            sent = short_call(
                order, live["prior"], blocks, halo, taps_full, live["mask"], step
            )
            flying["sent", step] = (step, sent)
    fence(last + 1)
    live.update({k: v for k, (_, v) in flying.items()})

    place = jnp.arange(2 * ctx_count, dtype=jnp.int32)
    dest = x_at * ctx_count + ctx_at
    dest = dest ^ ((place & 4) // 4 + (place & 2) * 2 + (place & 1) * 2)
    side = x_at.reshape(1)
    here = [live["here", j] for j in range(CHUNKS)]
    there = [live["there", j] for j in range(CHUNKS)]
    parts = []
    unit = half // QUARTERS
    for first, wide in PROJECTS:
        panels = []
        for kind in ("keep", "got"):
            for key in [k for k in live if isinstance(k, tuple) and len(k) == 3 and k[0] != "part"]:
                if key[0] == kind and key[1] <= first < key[1] + key[2]:
                    panels.append((live[key], (first - key[1]) * unit))
        if parts:
            here[0] = after(here[0], product)
        product = project_call(side, dest, here, there, panels, unit * wide, out_weight.shape[0])
        given = product.reshape(-1, tok_rows, product.shape[1])
        if parts:
            given = after(given, parts[-1])
        parts.append(lax.all_to_all(given, PLANE, split_axis=0, concat_axis=0, tiled=True))
    return place_call(parts, ctx_count)


def solution(mesh):
    count, ctx_count = mesh.devices.shape
    fine = Mesh(mesh.devices.reshape(count // 2, 2, ctx_count // 2, 2), EVERY)
    placed = (
        P(EVERY, None),
        P(EVERY, None),
        P(FSDP, None),
        P(),
        P(),
        P(FSDP, CTX),
    )
    return jax.shard_map(
        on_device, mesh=fine, in_specs=placed, out_specs=P(EVERY, None), check_vma=False
    )
```

```python
import functools

import jax
import jax.numpy as jnp
from jax import lax
from jax.experimental import pallas as pl
from jax.experimental.pallas import tpu as pltpu
from jax.sharding import Mesh
from jax.sharding import PartitionSpec as P

FSDP = ("fh", "fx")
CTX = ("y", "core")
PLANE = ("fx", "y", "core")
EVERY = ("fh", "fx", "y", "core")
SWAP = [(0, 1), (1, 0)]
CHUNKS = 4
QUARTERS = 4
PANEL_STEPS = (
    ("keep", 0, 2, 0, 2),
    ("got", 0, 2, 3, 5),
    ("both", 2, 2, 5, 20),
)
FENCED = 5
VIA_X = 3
NEAR_EARLY = (0, 1, 2)
PROJECTS = ((0, 2), (2, 2))
ROWS = 128
LANES = 128
MIB = 1 << 20
LIGHT = pl.CostEstimate(flops=1, bytes_accessed=1, transcendentals=0)


def short_kernel(order, order_prev, q, k, v, hq, hk, hv, fq, fk, fv, mask, out, ext):
    rows, wide = q.shape[1], q.shape[2]
    taps = hq.shape[1] + 1
    pad = 8
    linked = [jnp.broadcast_to(mask[0, :, i : i + 1], (rows, LANES)) for i in range(1, taps)]
    for first in range(0, wide, LANES):
        cols = slice(first, first + LANES)

        def conv(slot, block, halo, taps_ref):
            ext[slot, pad - (taps - 1) : pad] = halo[0, :, cols].astype(jnp.float32)
            own = block[0, :, cols].astype(jnp.float32)
            ext[slot, pad : pad + rows] = own
            total = taps_ref[0:1, cols] * own
            for i in range(1, taps):
                near = ext[slot, pad - i : pad - i + rows] * linked[i - 1]
                total = total + taps_ref[i : i + 1, cols] * near
            return total

        out[0, :, first : first + LANES] = conv(0, q, hq, fq).astype(jnp.bfloat16)
        gate = conv(1, k, hk, fk) * conv(2, v, hv, fv)
        out[0, :, wide + first : wide + first + LANES] = gate.astype(jnp.bfloat16)


def short_call(order, order_prev, blocks, halo, taps_full, mask, chunk):
    count, rows, wide = blocks.shape
    cols = wide // 3 // CHUNKS

    def of_block(part):
        return pl.BlockSpec((1, rows, cols), lambda g, o, p: (o[g], 0, part * CHUNKS + chunk))

    def of_halo(part):
        return pl.BlockSpec((1, halo.shape[1], cols), lambda g, o, p: (p[g], 0, part * (CHUNKS // 2) + chunk % (CHUNKS // 2)))

    def of_taps(part):
        return pl.BlockSpec((taps_full.shape[0], cols), lambda g, o, p: (0, part * CHUNKS + chunk))

    parts = range(3)
    return pl.pallas_call(
        short_kernel,
        grid_spec=pltpu.PrefetchScalarGridSpec(
            num_scalar_prefetch=2,
            grid=(count,),
            in_specs=[of_block(p) for p in parts]
            + [of_halo(p) for p in parts]
            + [of_taps(p) for p in parts]
            + [pl.BlockSpec((1,) + mask.shape[1:], lambda g, o, p: (g, 0, 0))],
            out_specs=pl.BlockSpec((1, rows, 2 * cols), lambda g, o, p: (g, 0, 0)),
            scratch_shapes=[pltpu.VMEM((3, 8 + rows, LANES), jnp.float32)],
        ),
        out_shape=jax.ShapeDtypeStruct((count, rows, 2 * cols), jnp.bfloat16),
        cost_estimate=LIGHT,
        name="short_conv",
    )(order, order_prev, blocks, blocks, blocks, halo, halo, halo, taps_full, taps_full, taps_full, mask)


def medium_kernel(group_size, q, gate, halo, taps, same, out):
    blocks = gate.shape[0] // ROWS
    lane = lax.broadcasted_iota(jnp.int32, (ROWS, LANES), 1) // group_size
    windows, totals = [], []
    for a in range(blocks):
        before = halo[...] if a == 0 else gate[(a - 1) * ROWS : a * ROWS]
        windows.append(jnp.concatenate([before, gate[a * ROWS : (a + 1) * ROWS]], axis=0))
        totals.append(jnp.zeros((ROWS, LANES), jnp.float32))
    for n in range(taps.shape[0]):
        row = jnp.broadcast_to(taps[n : n + 1], (ROWS, 2 * ROWS))
        matrix = pltpu.roll(row, 0, 1, stride=1, stride_axis=0).astype(jnp.bfloat16)
        for a in range(blocks):
            result = jnp.dot(matrix * same[a], windows[a], preferred_element_type=jnp.float32)
            totals[a] = jnp.where(lane == n, result, totals[a])
    for a in range(blocks):
        rows = slice(a * ROWS, (a + 1) * ROWS)
        out[rows] = (q[rows].astype(jnp.float32) * totals[a]).astype(jnp.bfloat16)


def medium_call(routed, halo, taps, same, chunk, group_size):
    rows, cols = routed.shape[0], routed.shape[1] // 2
    steps = cols // LANES
    groups = LANES // group_size
    return pl.pallas_call(
        functools.partial(medium_kernel, group_size),
        grid=(steps,),
        in_specs=[
            pl.BlockSpec((rows, LANES), lambda t: (0, t)),
            pl.BlockSpec((rows, LANES), lambda t: (0, steps + t)),
            pl.BlockSpec((ROWS, LANES), lambda t: (0, t)),
            pl.BlockSpec((groups, 2 * ROWS), lambda t: (chunk * steps + t, 0)),
            pl.BlockSpec(same.shape, lambda t: (0, 0, 0)),
        ],
        out_specs=pl.BlockSpec((rows, LANES), lambda t: (0, t)),
        out_shape=jax.ShapeDtypeStruct((rows, cols), jnp.bfloat16),
        cost_estimate=LIGHT,
        name="medium_conv",
    )(routed, routed, halo, taps, same)


def project_kernel(count, full, side, dest, *refs):
    pieces, panels, sums, out = refs[:count], refs[count : count + 2], refs[count + 2 : -1], refs[-1]
    held, depth = pieces[0].shape
    tile = out.shape[0] // dest.shape[0]
    for half in range(2):
        rows = slice(half * held, (half + 1) * held)
        total = sums[0][rows] if sums else None
        for m, piece in enumerate(pieces[half * count // 2 : (half + 1) * count // 2]):
            i, other = m // 2, m % 2
            term = jnp.dot(piece[...], panels[other][i], preferred_element_type=jnp.float32)
            total = term if total is None else total + term
        if not full:
            out[rows] = total
            continue
        total = total.astype(jnp.bfloat16)
        for m in range(held // tile):
            at = pl.multiple_of(dest[half * held // tile + m] * tile, tile)
            out[pl.ds(at, tile)] = total[m * tile : (m + 1) * tile]


def project_call(side, dest, here, there, panels, cols, depth, first, sums):
    held, wide = here[0].shape
    tile = min(256, cols)
    rows = len(here) * wide // 2 // depth
    full = first + len(here) == CHUNKS

    def specs():
        for i in range(wide // (2 * depth)):
            for other in range(2):
                yield pl.BlockSpec(
                    (held, depth),
                    lambda n, s, d, i=i, other=other: (0, 2 * i + (s[0] + other) % 2),
                    pipeline_mode=pl.Buffered(1),
                )

    at_rows = first * wide // 2 // depth // rows
    pieces = [x for x in list(here) + list(there) for _ in range(wide // depth)]
    given = [] if sums is None else [sums]
    return pl.pallas_call(
        functools.partial(project_kernel, len(pieces), full),
        grid_spec=pltpu.PrefetchScalarGridSpec(
            num_scalar_prefetch=2,
            grid=(cols // tile,),
            in_specs=[spec for _ in list(here) + list(there) for spec in specs()]
            + [
                pl.BlockSpec(
                    (rows, depth, tile), lambda n, s, d, row=row, at=at // tile: (at_rows, row, at + n)
                )
                for _, row, at in panels
            ]
            + [pl.BlockSpec((2 * held, tile), lambda n, s, d: (0, n)) for _ in given],
            out_specs=pl.BlockSpec((2 * held, tile), lambda n, s, d: (0, n)),
        ),
        out_shape=jax.ShapeDtypeStruct((2 * held, cols), jnp.bfloat16 if full else jnp.float32),
        compiler_params=pltpu.CompilerParams(vmem_limit_bytes=56 * MIB),
        cost_estimate=LIGHT,
        name="project",
    )(side, dest, *pieces, *(p for p, _, _ in panels), *given)


def stack_kernel(*refs):
    out = refs[-1]
    rows = refs[0].shape[0]
    for m, piece in enumerate(refs[:-1]):
        out[m * rows : (m + 1) * rows] = piece[...]


def stack_call(pieces):
    rows, cols = pieces[0].shape
    tile = min(256, cols)
    return pl.pallas_call(
        stack_kernel,
        grid=(cols // tile,),
        in_specs=[pl.BlockSpec((rows, tile), lambda n: (0, n)) for _ in pieces],
        out_specs=pl.BlockSpec((len(pieces) * rows, tile), lambda n: (0, n)),
        out_shape=jax.ShapeDtypeStruct((len(pieces) * rows, cols), pieces[0].dtype),
        cost_estimate=LIGHT,
        name="stack",
    )(*pieces)


def place_kernel(*refs):
    out, at = refs[-1], 0
    for part in refs[:-1]:
        out[:, at : at + part.shape[2]] = part[0]
        at += part.shape[2]


def place_call(parts, ctx_count):
    count, rows = parts[0].shape[:2]
    wide = sum(p.shape[2] for p in parts)
    return pl.pallas_call(
        place_kernel,
        grid=(count,),
        in_specs=[pl.BlockSpec((1, rows, p.shape[2]), lambda s: (s, 0, 0)) for p in parts],
        out_specs=pl.BlockSpec(
            (rows, wide), lambda s: (0, (s % ctx_count) * (count // ctx_count) + s // ctx_count)
        ),
        out_shape=jax.ShapeDtypeStruct((rows, count * wide), parts[0].dtype),
        compiler_params=pltpu.CompilerParams(vmem_limit_bytes=16 * MIB),
        cost_estimate=LIGHT,
        name="place",
    )(*parts)


def after(value, *others):
    return lax.optimization_barrier((value,) + others)[0]


def on_device(loaded, route, doc_ids, short_filter, medium_filter, out_weight):
    tok_rows, wide = loaded.shape
    channels = wide // 3
    count = lax.axis_size(FSDP)
    ctx_count = lax.axis_size(CTX)
    blk = tok_rows // count
    short_len = short_filter.shape[0]
    depth = short_len - 1
    medium_len = medium_filter.shape[0]
    group_size = wide // short_filter.shape[1]
    length = doc_ids.shape[1]
    cols = channels // CHUNKS
    ctx_at = lax.axis_index(CTX)
    f_at = lax.axis_index(FSDP)
    x_at = lax.axis_index("fx")

    shift = []
    for f in range(count):
        for c in range(ctx_count):
            if f + 1 < count:
                shift.append((f * ctx_count + c, (f + 1) * ctx_count + c))
            elif c + 1 < ctx_count:
                shift.append((f * ctx_count + c, c + 1))

    onward = [(i - ctx_count, o) for i, o in shift if i // ctx_count % 2 == 1]

    live, flying = {}, {}

    seqs = jnp.arange(count, dtype=jnp.int32)
    order = jnp.sum(jnp.where(route[0][None, :] == seqs[:, None], seqs[None, :], 0), axis=1)
    blocks = loaded.reshape(count, blk, wide)
    tails = []
    for i in range(2):
        parts = [
            blocks[:, blk - depth :, at : at + channels // 2]
            for at in range(i * channels // 2, wide, channels)
        ]
        tails.append(jnp.concatenate(parts, axis=2).reshape(count * depth, wide // 2))
    direct = lax.ppermute(tails[0], EVERY, shift).reshape(count, depth, wide // 2)

    own_ids = jnp.concatenate([jnp.full((depth,), -1, jnp.int32), doc_ids[0]])
    own_ids = lax.dynamic_slice_in_dim(own_ids, ctx_at * tok_rows, depth + tok_rows, 0)
    near = jnp.stack([own_ids[f * blk : (f + 1) * blk + depth] for f in range(count)])
    order_prev = lax.ppermute(after(order, tails[0]), EVERY, shift)
    near = after(near, tails[0])
    near = lax.all_to_all(near, FSDP, split_axis=0, concat_axis=0, tiled=True)


    taps_full = jnp.repeat(short_filter, group_size, axis=1)

    half = out_weight.shape[1] // 2
    keep = lax.dynamic_slice_in_dim(after(out_weight, tails[0]), x_at * half, half, 1)
    give = lax.dynamic_slice_in_dim(out_weight, (1 - x_at) * half, half, 1)

    reach = ROWS - medium_len
    medium_rows = jnp.pad(
        medium_filter.astype(jnp.float32)[::-1].T, ((0, 0), (reach + 1, ROWS - 1))
    )
    own = jnp.concatenate([jnp.full((ROWS,), -1, jnp.int32), doc_ids[0]])
    own = lax.dynamic_slice_in_dim(own, ctx_at * tok_rows, ROWS + tok_rows, 0)
    same = jnp.stack(
        [
            own[ROWS + a : 2 * ROWS + a][:, None] == own[a : 2 * ROWS + a][None, :]
            for a in range(0, tok_rows, ROWS)
        ]
    ).astype(jnp.bfloat16)

    next_ctx = [(c, c + 1) for c in range(ctx_count - 1)]

    def exchange(sent):
        routed = lax.all_to_all(sent, FSDP, split_axis=0, concat_axis=0, tiled=True)
        return routed.reshape(tok_rows, 2 * cols)

    def cut(kind, first, wide):
        at = half // QUARTERS * first
        return live[kind][:, at : at + half // QUARTERS * wide]

    def fence(step):
        for key in [k for k, (due, _) in flying.items() if due <= step]:
            live[key] = flying.pop(key)[1]
        if step > FENCED:
            return
        keys = list(live)
        for key, value in zip(keys, lax.optimization_barrier([live[k] for k in keys])):
            live[key] = value

    def start_panels(step):
        for kind, first, wide, begin, due in PANEL_STEPS:
            if begin == step:
                kinds = ("keep", "got") if kind == "both" else (kind,)
                part = jnp.concatenate([cut(k, first, wide) for k in kinds], axis=0)
                flying[kind, first, wide] = (due, lax.all_gather(part[None], "fh", axis=0, tiled=True))

    live["keep"] = keep
    start_panels(0)
    direct, near, order_prev = lax.optimization_barrier((direct, near, order_prev))
    mask = jnp.stack(
        [near[:, depth - i : depth - i + blk] == near[:, depth:] for i in range(short_len)], axis=-1
    ).astype(jnp.float32)
    live["give"] = give
    turned = lax.ppermute(after(tails[1], tails[0]), "fx", SWAP)
    passed = lax.ppermute(turned, EVERY, onward)
    flying["halo"] = (2, jnp.where(x_at == 1, turned, passed).reshape(count, depth, wide // 2))
    live["sent", 0] = short_call(order, order_prev, blocks, direct, taps_full, mask, 0)
    live["mask"] = mask
    live["prior"] = order_prev
    live["medium"] = medium_rows
    live["same"] = same
    place = jnp.arange(2 * ctx_count, dtype=jnp.int32)
    dest = x_at * ctx_count + ctx_at
    dest = dest ^ ((place & 4) // 4 + (place & 2) * 2 + (place & 1) * 2)
    side = x_at.reshape(1)
    unit = half // QUARTERS

    def project(low, high, first, wide, sums=None):
        held = {**live, **{k: v for k, (_, v) in flying.items()}}
        panels = []
        for other, kind in enumerate(("keep", "got")):
            for key in [k for k in held if isinstance(k, tuple) and len(k) == 3 and k[0] in (kind, "both")]:
                if key[1] <= first < key[1] + key[2]:
                    row = other if key[0] == "both" else 0
                    panels.append((held[key], row, (first - key[1]) * unit))
        here, there = ([held[k, j] for j in range(low, high)] for k in ("here", "there"))
        depth = out_weight.shape[0]
        return project_call(side, dest, here, there, panels, unit * wide, depth, low, sums)

    newest = []

    def stack_steps(step, j):
        if FENCED <= step and j < CHUNKS - 1:
            live["gated", j] = after(live["gated", j], live["by_x", CHUNKS - 1])
        here = stack_call([live.pop((k, j)) for k in ("gated", "by_y", "by_x", "by_both")])
        flying["here", j] = (step, here)
        flying["there", j] = (step + 1, lax.ppermute(here, "core", SWAP))

    last = CHUNKS + 4
    for step in range(1, last + 1):
        fence(step)
        start_panels(step)
        if step == 1:
            flying["got"] = (2, lax.ppermute(live.pop("give"), "fx", SWAP))
        if step <= CHUNKS:
            flying["routed", step - 1] = (step, exchange(live.pop(("sent", step - 1))))
        for j in [j for j in range(CHUNKS) if step == j + 4 - (j in NEAR_EARLY)]:
            first, second = ("by_x", "y") if j < VIA_X else ("by_y", "fx")
            flying["by_both", j] = (step, lax.ppermute(live[first, j], second, SWAP))
        j = step - 3
        if 0 <= j < CHUNKS and j not in NEAR_EARLY:
            live["gated", j] = after(live["gated", j], live["by_both", j - 1])
            flying["by_x", j] = (step, lax.ppermute(live["gated", j], "fx", SWAP))
            flying["by_y", j] = (step, lax.ppermute(live["gated", j], "y", SWAP))
        j = step - 2
        if 0 <= j < CHUNKS:
            routed = live.pop(("routed", j))
            before = lax.ppermute(routed[tok_rows - ROWS :, cols:], CTX, next_ctx)
            gated = medium_call(routed, before, live["medium"], live["same"], j, group_size)
            flying["gated", j] = (step, gated)
            newest.append(gated)
            if j in NEAR_EARLY:
                flying["by_x", j] = (step, lax.ppermute(gated, "fx", SWAP))
                flying["by_y", j] = (step, lax.ppermute(gated, "y", SWAP))
        for j in [j for j in range(CHUNKS) if step == (4, 7, 7, 8)[j]]:
            stack_steps(step, j)
        if step < CHUNKS:
            halo = direct if step < CHUNKS // 2 else live["halo"]
            sent = short_call(order, live["prior"], blocks, halo, taps_full, live["mask"], step)
            flying["sent", step] = (step, sent)
    fence(last + 1)
    live.update({k: v for k, (_, v) in flying.items()})

    parts, product = [], None
    for n, (first, wide) in enumerate(PROJECTS):
        if n > 0:
            live["here", 0] = after(live["here", 0], product)
        product = project(0, CHUNKS, first, wide)
        given = product.reshape(-1, tok_rows, product.shape[1])
        if parts:
            given = after(given, parts[-1])
        parts.append(lax.all_to_all(given, PLANE, split_axis=0, concat_axis=0, tiled=True))
    return place_call(parts, ctx_count)


def solution(mesh):
    count, ctx_count = mesh.devices.shape
    fine = Mesh(mesh.devices.reshape(count // 2, 2, ctx_count // 2, 2), EVERY)
    placed = (
        P(EVERY, None),
        P(EVERY, None),
        P(FSDP, None),
        P(),
        P(),
        P(FSDP, CTX),
    )
    return jax.shard_map(
        on_device, mesh=fine, in_specs=placed, out_specs=P(EVERY, None), check_vma=False
    )
```

```python
import functools

import jax
import jax.numpy as jnp
from jax import lax
from jax.experimental import pallas as pl
from jax.experimental.pallas import tpu as pltpu
from jax.sharding import Mesh
from jax.sharding import PartitionSpec as P

FSDP = ("fh", "fx")
CTX = ("y", "core")
PLANE = ("fx", "y", "core")
EVERY = ("fh", "fx", "y", "core")
SWAP = [(0, 1), (1, 0)]
CHUNKS = 4
QUARTERS = 4
PANEL_STEPS = (
    ("keep", 0, 2, 0, 2),
    ("got", 0, 2, 3, 5),
    ("both", 2, 2, 5, 20),
)
FENCED = 5
VIA_X = 3
NEAR_EARLY = (0, 1, 2)
PROJECTS = ((0, 2), (2, 2))
ROWS = 128
LANES = 128
MIB = 1 << 20
LIGHT = pl.CostEstimate(flops=1, bytes_accessed=1, transcendentals=0)


def short_kernel(order, order_prev, q, k, v, hq, hk, hv, fq, fk, fv, mask, out, ext):
    rows, wide = q.shape[1], q.shape[2]
    taps = hq.shape[1] + 1
    pad = 8
    linked = [jnp.broadcast_to(mask[0, :, i : i + 1], (rows, LANES)) for i in range(1, taps)]
    for first in range(0, wide, LANES):
        cols = slice(first, first + LANES)

        def conv(slot, block, halo, taps_ref):
            ext[slot, pad - (taps - 1) : pad] = halo[0, :, cols].astype(jnp.float32)
            own = block[0, :, cols].astype(jnp.float32)
            ext[slot, pad : pad + rows] = own
            total = taps_ref[0:1, cols] * own
            for i in range(1, taps):
                near = ext[slot, pad - i : pad - i + rows] * linked[i - 1]
                total = total + taps_ref[i : i + 1, cols] * near
            return total

        out[0, :, first : first + LANES] = conv(0, q, hq, fq).astype(jnp.bfloat16)
        gate = conv(1, k, hk, fk) * conv(2, v, hv, fv)
        out[0, :, wide + first : wide + first + LANES] = gate.astype(jnp.bfloat16)


def short_call(order, order_prev, blocks, halo, taps_full, mask, chunk):
    count, rows, wide = blocks.shape
    cols = wide // 3 // CHUNKS

    def of_block(part):
        return pl.BlockSpec((1, rows, cols), lambda g, o, p: (o[g], 0, part * CHUNKS + chunk))

    def of_halo(part):
        return pl.BlockSpec((1, halo.shape[1], cols), lambda g, o, p: (p[g], 0, part * (CHUNKS // 2) + chunk % (CHUNKS // 2)))

    def of_taps(part):
        return pl.BlockSpec((taps_full.shape[0], cols), lambda g, o, p: (0, part * CHUNKS + chunk))

    parts = range(3)
    return pl.pallas_call(
        short_kernel,
        grid_spec=pltpu.PrefetchScalarGridSpec(
            num_scalar_prefetch=2,
            grid=(count,),
            in_specs=[of_block(p) for p in parts]
            + [of_halo(p) for p in parts]
            + [of_taps(p) for p in parts]
            + [pl.BlockSpec((1,) + mask.shape[1:], lambda g, o, p: (g, 0, 0))],
            out_specs=pl.BlockSpec((1, rows, 2 * cols), lambda g, o, p: (g, 0, 0)),
            scratch_shapes=[pltpu.VMEM((3, 8 + rows, LANES), jnp.float32)],
        ),
        out_shape=jax.ShapeDtypeStruct((count, rows, 2 * cols), jnp.bfloat16),
        cost_estimate=LIGHT,
        name="short_conv",
    )(order, order_prev, blocks, blocks, blocks, halo, halo, halo, taps_full, taps_full, taps_full, mask)


def medium_kernel(group_size, q, gate, halo, taps, same, out):
    blocks = gate.shape[0] // ROWS
    lane = lax.broadcasted_iota(jnp.int32, (ROWS, LANES), 1) // group_size
    windows, totals = [], []
    for a in range(blocks):
        before = halo[...] if a == 0 else gate[(a - 1) * ROWS : a * ROWS]
        windows.append(jnp.concatenate([before, gate[a * ROWS : (a + 1) * ROWS]], axis=0))
        totals.append(jnp.zeros((ROWS, LANES), jnp.float32))
    for n in range(taps.shape[0]):
        row = jnp.broadcast_to(taps[n : n + 1], (ROWS, 2 * ROWS))
        matrix = pltpu.roll(row, 0, 1, stride=1, stride_axis=0).astype(jnp.bfloat16)
        for a in range(blocks):
            result = jnp.dot(matrix * same[a], windows[a], preferred_element_type=jnp.float32)
            totals[a] = jnp.where(lane == n, result, totals[a])
    for a in range(blocks):
        rows = slice(a * ROWS, (a + 1) * ROWS)
        out[rows] = (q[rows].astype(jnp.float32) * totals[a]).astype(jnp.bfloat16)


def medium_call(routed, halo, taps, same, chunk, group_size):
    rows, cols = routed.shape[0], routed.shape[1] // 2
    steps = cols // LANES
    groups = LANES // group_size
    return pl.pallas_call(
        functools.partial(medium_kernel, group_size),
        grid=(steps,),
        in_specs=[
            pl.BlockSpec((rows, LANES), lambda t: (0, t)),
            pl.BlockSpec((rows, LANES), lambda t: (0, steps + t)),
            pl.BlockSpec((ROWS, LANES), lambda t: (0, t)),
            pl.BlockSpec((groups, 2 * ROWS), lambda t: (chunk * steps + t, 0)),
            pl.BlockSpec(same.shape, lambda t: (0, 0, 0)),
        ],
        out_specs=pl.BlockSpec((rows, LANES), lambda t: (0, t)),
        out_shape=jax.ShapeDtypeStruct((rows, cols), jnp.bfloat16),
        cost_estimate=LIGHT,
        name="medium_conv",
    )(routed, routed, halo, taps, same)


def project_kernel(count, full, side, dest, *refs):
    pieces, panels, sums, out = refs[:count], refs[count : count + 2], refs[count + 2 : -1], refs[-1]
    held, depth = pieces[0].shape
    tile = out.shape[0] // dest.shape[0]
    for half in range(2):
        rows = slice(half * held, (half + 1) * held)
        total = sums[0][rows] if sums else None
        for m, piece in enumerate(pieces[half * count // 2 : (half + 1) * count // 2]):
            i, other = m // 2, m % 2
            term = jnp.dot(piece[...], panels[other][i], preferred_element_type=jnp.float32)
            total = term if total is None else total + term
        if not full:
            out[rows] = total
            continue
        total = total.astype(jnp.bfloat16)
        for m in range(held // tile):
            at = pl.multiple_of(dest[half * held // tile + m] * tile, tile)
            out[pl.ds(at, tile)] = total[m * tile : (m + 1) * tile]


def project_call(side, dest, here, there, panels, cols, depth, first, sums):
    held, wide = here[0].shape
    tile = min(256, cols)
    rows = len(here) * wide // 2 // depth
    full = first + len(here) == CHUNKS

    def specs():
        for i in range(wide // (2 * depth)):
            for other in range(2):
                yield pl.BlockSpec(
                    (held, depth),
                    lambda n, s, d, i=i, other=other: (0, 2 * i + (s[0] + other) % 2),
                    pipeline_mode=pl.Buffered(1),
                )

    at_rows = first * wide // 2 // depth // rows
    pieces = [x for x in list(here) + list(there) for _ in range(wide // depth)]
    given = [] if sums is None else [sums]
    return pl.pallas_call(
        functools.partial(project_kernel, len(pieces), full),
        grid_spec=pltpu.PrefetchScalarGridSpec(
            num_scalar_prefetch=2,
            grid=(cols // tile,),
            in_specs=[spec for _ in list(here) + list(there) for spec in specs()]
            + [
                pl.BlockSpec(
                    (rows, depth, tile), lambda n, s, d, row=row, at=at // tile: (at_rows, row, at + n)
                )
                for _, row, at in panels
            ]
            + [pl.BlockSpec((2 * held, tile), lambda n, s, d: (0, n)) for _ in given],
            out_specs=pl.BlockSpec((2 * held, tile), lambda n, s, d: (0, n)),
        ),
        out_shape=jax.ShapeDtypeStruct((2 * held, cols), jnp.bfloat16 if full else jnp.float32),
        compiler_params=pltpu.CompilerParams(vmem_limit_bytes=56 * MIB),
        cost_estimate=LIGHT,
        name="project",
    )(side, dest, *pieces, *(p for p, _, _ in panels), *given)


def stack_kernel(*refs):
    out = refs[-1]
    rows = refs[0].shape[0]
    for m, piece in enumerate(refs[:-1]):
        out[m * rows : (m + 1) * rows] = piece[...]


def stack_call(pieces):
    rows, cols = pieces[0].shape
    tile = min(256, cols)
    return pl.pallas_call(
        stack_kernel,
        grid=(cols // tile,),
        in_specs=[pl.BlockSpec((rows, tile), lambda n: (0, n)) for _ in pieces],
        out_specs=pl.BlockSpec((len(pieces) * rows, tile), lambda n: (0, n)),
        out_shape=jax.ShapeDtypeStruct((len(pieces) * rows, cols), pieces[0].dtype),
        cost_estimate=LIGHT,
        name="stack",
    )(*pieces)


def place_kernel(*refs):
    out, at = refs[-1], 0
    for part in refs[:-1]:
        out[:, at : at + part.shape[2]] = part[0]
        at += part.shape[2]


def place_call(parts, ctx_count):
    count, rows = parts[0].shape[:2]
    wide = sum(p.shape[2] for p in parts)
    return pl.pallas_call(
        place_kernel,
        grid=(count,),
        in_specs=[pl.BlockSpec((1, rows, p.shape[2]), lambda s: (s, 0, 0)) for p in parts],
        out_specs=pl.BlockSpec(
            (rows, wide), lambda s: (0, (s % ctx_count) * (count // ctx_count) + s // ctx_count)
        ),
        out_shape=jax.ShapeDtypeStruct((rows, count * wide), parts[0].dtype),
        compiler_params=pltpu.CompilerParams(vmem_limit_bytes=16 * MIB),
        cost_estimate=LIGHT,
        name="place",
    )(*parts)


def after(value, *others):
    return lax.optimization_barrier((value,) + others)[0]


def on_device(loaded, route, doc_ids, short_filter, medium_filter, out_weight):
    tok_rows, wide = loaded.shape
    channels = wide // 3
    count = lax.axis_size(FSDP)
    ctx_count = lax.axis_size(CTX)
    blk = tok_rows // count
    short_len = short_filter.shape[0]
    depth = short_len - 1
    medium_len = medium_filter.shape[0]
    group_size = wide // short_filter.shape[1]
    length = doc_ids.shape[1]
    cols = channels // CHUNKS
    ctx_at = lax.axis_index(CTX)
    f_at = lax.axis_index(FSDP)
    x_at = lax.axis_index("fx")

    shift = []
    for f in range(count):
        for c in range(ctx_count):
            if f + 1 < count:
                shift.append((f * ctx_count + c, (f + 1) * ctx_count + c))
            elif c + 1 < ctx_count:
                shift.append((f * ctx_count + c, c + 1))

    live, flying = {}, {}

    seqs = jnp.arange(count, dtype=jnp.int32)
    order = jnp.sum(jnp.where(route[0][None, :] == seqs[:, None], seqs[None, :], 0), axis=1)
    blocks = loaded.reshape(count, blk, wide)
    tails = []
    for i in range(2):
        parts = [
            blocks[:, blk - depth :, at : at + channels // 2]
            for at in range(i * channels // 2, wide, channels)
        ]
        tails.append(jnp.concatenate(parts, axis=2).reshape(count * depth, wide // 2))
    direct = lax.ppermute(tails[0], EVERY, shift).reshape(count, depth, wide // 2)

    own_ids = jnp.concatenate([jnp.full((depth,), -1, jnp.int32), doc_ids[0]])
    own_ids = lax.dynamic_slice_in_dim(own_ids, ctx_at * tok_rows, depth + tok_rows, 0)
    near = jnp.stack([own_ids[f * blk : (f + 1) * blk + depth] for f in range(count)])
    order_prev = lax.ppermute(after(order, tails[0]), EVERY, shift)
    near = after(near, tails[0])
    near = lax.all_to_all(near, FSDP, split_axis=0, concat_axis=0, tiled=True)


    taps_full = jnp.repeat(short_filter, group_size, axis=1)

    half = out_weight.shape[1] // 2
    keep = lax.dynamic_slice_in_dim(after(out_weight, tails[0]), x_at * half, half, 1)
    give = lax.dynamic_slice_in_dim(out_weight, (1 - x_at) * half, half, 1)

    reach = ROWS - medium_len
    medium_rows = jnp.pad(
        medium_filter.astype(jnp.float32)[::-1].T, ((0, 0), (reach + 1, ROWS - 1))
    )
    own = jnp.concatenate([jnp.full((ROWS,), -1, jnp.int32), doc_ids[0]])
    own = lax.dynamic_slice_in_dim(own, ctx_at * tok_rows, ROWS + tok_rows, 0)
    same = jnp.stack(
        [
            own[ROWS + a : 2 * ROWS + a][:, None] == own[a : 2 * ROWS + a][None, :]
            for a in range(0, tok_rows, ROWS)
        ]
    ).astype(jnp.bfloat16)

    next_ctx = [(c, c + 1) for c in range(ctx_count - 1)]

    def exchange(sent):
        routed = lax.all_to_all(sent, FSDP, split_axis=0, concat_axis=0, tiled=True)
        return routed.reshape(tok_rows, 2 * cols)

    def cut(kind, first, wide):
        at = half // QUARTERS * first
        return live[kind][:, at : at + half // QUARTERS * wide]

    def fence(step):
        for key in [k for k, (due, _) in flying.items() if due <= step]:
            live[key] = flying.pop(key)[1]
        if step > FENCED:
            return
        keys = list(live)
        for key, value in zip(keys, lax.optimization_barrier([live[k] for k in keys])):
            live[key] = value

    def start_panels(step):
        for kind, first, wide, begin, due in PANEL_STEPS:
            if begin == step:
                kinds = ("keep", "got") if kind == "both" else (kind,)
                part = jnp.concatenate([cut(k, first, wide) for k in kinds], axis=0)
                flying[kind, first, wide] = (due, lax.all_gather(part[None], "fh", axis=0, tiled=True))

    live["keep"] = keep
    start_panels(0)
    direct, near, order_prev = lax.optimization_barrier((direct, near, order_prev))
    mask = jnp.stack(
        [near[:, depth - i : depth - i + blk] == near[:, depth:] for i in range(short_len)], axis=-1
    ).astype(jnp.float32)
    live["give"] = give
    rest = lax.ppermute(after(tails[1], tails[0]), EVERY, shift).reshape(count, depth, wide // 2)
    flying["halo"] = (2, rest)
    live["sent", 0] = short_call(order, order_prev, blocks, direct, taps_full, mask, 0)
    live["mask"] = mask
    live["prior"] = order_prev
    live["medium"] = medium_rows
    live["same"] = same
    place = jnp.arange(2 * ctx_count, dtype=jnp.int32)
    dest = x_at * ctx_count + ctx_at
    dest = dest ^ ((place & 4) // 4 + (place & 2) * 2 + (place & 1) * 2)
    side = x_at.reshape(1)
    unit = half // QUARTERS

    def project(low, high, first, wide, sums=None):
        held = {**live, **{k: v for k, (_, v) in flying.items()}}
        panels = []
        for other, kind in enumerate(("keep", "got")):
            for key in [k for k in held if isinstance(k, tuple) and len(k) == 3 and k[0] in (kind, "both")]:
                if key[1] <= first < key[1] + key[2]:
                    row = other if key[0] == "both" else 0
                    panels.append((held[key], row, (first - key[1]) * unit))
        here, there = ([held[k, j] for j in range(low, high)] for k in ("here", "there"))
        depth = out_weight.shape[0]
        return project_call(side, dest, here, there, panels, unit * wide, depth, low, sums)


    def stack_steps(step, j):
        if FENCED <= step and j < CHUNKS - 1:
            live["gated", j] = after(live["gated", j], live["by_x", CHUNKS - 1])
        here = stack_call([live.pop((k, j)) for k in ("gated", "by_y", "by_x", "by_both")])
        flying["here", j] = (step, here)
        flying["there", j] = (step + 1, lax.ppermute(here, "core", SWAP))

    last = CHUNKS + 4
    for step in range(1, last + 1):
        fence(step)
        start_panels(step)
        if step == 1:
            flying["got"] = (2, lax.ppermute(live.pop("give"), "fx", SWAP))
        if step <= CHUNKS:
            flying["routed", step - 1] = (step, exchange(live.pop(("sent", step - 1))))
        for j in [j for j in range(CHUNKS) if step == j + 4 - (j in NEAR_EARLY)]:
            if j < VIA_X:
                flying["by_both", j] = (step, lax.ppermute(live["by_x", j], "y", SWAP))
        j = step - 3
        if 0 <= j < CHUNKS and j not in NEAR_EARLY:
            live["gated", j] = after(live["gated", j], live["by_both", j - 1])
            flying["by_x", j] = (step, lax.ppermute(live["gated", j], "fx", SWAP))
            flying["by_y", j] = (step, lax.ppermute(live["gated", j], "y", SWAP))
            across = [(0, 3), (1, 2), (2, 1), (3, 0)]
            flying["by_both", j] = (step, lax.ppermute(live["gated", j], ("fx", "y"), across))
        j = step - 2
        if 0 <= j < CHUNKS:
            routed = live.pop(("routed", j))
            before = lax.ppermute(routed[tok_rows - ROWS :, cols:], CTX, next_ctx)
            gated = medium_call(routed, before, live["medium"], live["same"], j, group_size)
            flying["gated", j] = (step, gated)
            if j in NEAR_EARLY:
                flying["by_x", j] = (step, lax.ppermute(gated, "fx", SWAP))
                flying["by_y", j] = (step, lax.ppermute(gated, "y", SWAP))
        for j in [j for j in range(CHUNKS) if step == (4, 7, 7, 8)[j]]:
            stack_steps(step, j)
        if step < CHUNKS:
            halo = direct if step < CHUNKS // 2 else live["halo"]
            sent = short_call(order, live["prior"], blocks, halo, taps_full, live["mask"], step)
            flying["sent", step] = (step, sent)
    fence(last + 1)
    live.update({k: v for k, (_, v) in flying.items()})

    parts, product = [], None
    for n, (first, wide) in enumerate(PROJECTS):
        if n > 0:
            live["here", 0] = after(live["here", 0], product)
        product = project(0, CHUNKS, first, wide)
        given = product.reshape(-1, tok_rows, product.shape[1])
        if parts:
            given = after(given, parts[-1])
        parts.append(lax.all_to_all(given, PLANE, split_axis=0, concat_axis=0, tiled=True))
    return place_call(parts, ctx_count)


def solution(mesh):
    count, ctx_count = mesh.devices.shape
    fine = Mesh(mesh.devices.reshape(count // 2, 2, ctx_count // 2, 2), EVERY)
    placed = (
        P(EVERY, None),
        P(EVERY, None),
        P(FSDP, None),
        P(),
        P(),
        P(FSDP, CTX),
    )
    return jax.shard_map(
        on_device, mesh=fine, in_specs=placed, out_specs=P(EVERY, None), check_vma=False
    )
```

```python
import functools

import jax
import jax.numpy as jnp
from jax import lax
from jax.experimental import pallas as pl
from jax.experimental.pallas import tpu as pltpu
from jax.sharding import Mesh
from jax.sharding import PartitionSpec as P

FSDP = ("fh", "fx")
CTX = ("y", "core")
PLANE = ("fx", "y", "core")
EVERY = ("fh", "fx", "y", "core")
SWAP = [(0, 1), (1, 0)]
CHUNKS = 4
QUARTERS = 4
PANEL_STEPS = (
    ("keep", 0, 2, 0, 2),
    ("got", 0, 2, 3, 5),
    ("both", 2, 2, 5, 20),
)
FENCED = 5
VIA_X = 3
NEAR_EARLY = (0, 1, 2)
PROJECTS = ((0, 2), (2, 2))
ROWS = 128
LANES = 128
MIB = 1 << 20
LIGHT = pl.CostEstimate(flops=1, bytes_accessed=1, transcendentals=0)


def short_kernel(order, order_prev, q, k, v, hq, hk, hv, fq, fk, fv, mask, out, ext):
    rows, wide = q.shape[1], q.shape[2]
    taps = hq.shape[1] + 1
    pad = 8
    linked = [jnp.broadcast_to(mask[0, :, i : i + 1], (rows, LANES)) for i in range(1, taps)]
    for first in range(0, wide, LANES):
        cols = slice(first, first + LANES)

        def conv(slot, block, halo, taps_ref):
            ext[slot, pad - (taps - 1) : pad] = halo[0, :, cols].astype(jnp.float32)
            own = block[0, :, cols].astype(jnp.float32)
            ext[slot, pad : pad + rows] = own
            total = taps_ref[0:1, cols] * own
            for i in range(1, taps):
                near = ext[slot, pad - i : pad - i + rows] * linked[i - 1]
                total = total + taps_ref[i : i + 1, cols] * near
            return total

        out[0, :, first : first + LANES] = conv(0, q, hq, fq).astype(jnp.bfloat16)
        gate = conv(1, k, hk, fk) * conv(2, v, hv, fv)
        out[0, :, wide + first : wide + first + LANES] = gate.astype(jnp.bfloat16)


def short_call(order, order_prev, blocks, halo, taps_full, mask, chunk):
    count, rows, wide = blocks.shape
    cols = wide // 3 // CHUNKS

    def of_block(part):
        return pl.BlockSpec((1, rows, cols), lambda g, o, p: (o[g], 0, part * CHUNKS + chunk))

    def of_halo(part):
        return pl.BlockSpec((1, halo.shape[1], cols), lambda g, o, p: (p[g], 0, part * (CHUNKS // 2) + chunk % (CHUNKS // 2)))

    def of_taps(part):
        return pl.BlockSpec((taps_full.shape[0], cols), lambda g, o, p: (0, part * CHUNKS + chunk))

    parts = range(3)
    return pl.pallas_call(
        short_kernel,
        grid_spec=pltpu.PrefetchScalarGridSpec(
            num_scalar_prefetch=2,
            grid=(count,),
            in_specs=[of_block(p) for p in parts]
            + [of_halo(p) for p in parts]
            + [of_taps(p) for p in parts]
            + [pl.BlockSpec((1,) + mask.shape[1:], lambda g, o, p: (g, 0, 0))],
            out_specs=pl.BlockSpec((1, rows, 2 * cols), lambda g, o, p: (g, 0, 0)),
            scratch_shapes=[pltpu.VMEM((3, 8 + rows, LANES), jnp.float32)],
        ),
        out_shape=jax.ShapeDtypeStruct((count, rows, 2 * cols), jnp.bfloat16),
        cost_estimate=LIGHT,
        name="short_conv",
    )(order, order_prev, blocks, blocks, blocks, halo, halo, halo, taps_full, taps_full, taps_full, mask)


def medium_kernel(group_size, q, gate, halo, taps, same, out):
    blocks = gate.shape[0] // ROWS
    lane = lax.broadcasted_iota(jnp.int32, (ROWS, LANES), 1) // group_size
    windows, totals = [], []
    for a in range(blocks):
        before = halo[...] if a == 0 else gate[(a - 1) * ROWS : a * ROWS]
        windows.append(jnp.concatenate([before, gate[a * ROWS : (a + 1) * ROWS]], axis=0))
        totals.append(jnp.zeros((ROWS, LANES), jnp.float32))
    for n in range(taps.shape[0]):
        row = jnp.broadcast_to(taps[n : n + 1], (ROWS, 2 * ROWS))
        matrix = pltpu.roll(row, 0, 1, stride=1, stride_axis=0).astype(jnp.bfloat16)
        for a in range(blocks):
            result = jnp.dot(matrix * same[a], windows[a], preferred_element_type=jnp.float32)
            totals[a] = jnp.where(lane == n, result, totals[a])
    for a in range(blocks):
        rows = slice(a * ROWS, (a + 1) * ROWS)
        out[rows] = (q[rows].astype(jnp.float32) * totals[a]).astype(jnp.bfloat16)


def medium_call(routed, halo, taps, same, chunk, group_size):
    rows, cols = routed.shape[0], routed.shape[1] // 2
    steps = cols // LANES
    groups = LANES // group_size
    return pl.pallas_call(
        functools.partial(medium_kernel, group_size),
        grid=(steps,),
        in_specs=[
            pl.BlockSpec((rows, LANES), lambda t: (0, t)),
            pl.BlockSpec((rows, LANES), lambda t: (0, steps + t)),
            pl.BlockSpec((ROWS, LANES), lambda t: (0, t)),
            pl.BlockSpec((groups, 2 * ROWS), lambda t: (chunk * steps + t, 0)),
            pl.BlockSpec(same.shape, lambda t: (0, 0, 0)),
        ],
        out_specs=pl.BlockSpec((rows, LANES), lambda t: (0, t)),
        out_shape=jax.ShapeDtypeStruct((rows, cols), jnp.bfloat16),
        cost_estimate=LIGHT,
        name="medium_conv",
    )(routed, routed, halo, taps, same)


def project_kernel(count, depth, side, dest, *refs):
    pieces, panels, (out, held, sems) = refs[:count], refs[count : count + 2], refs[count + 2 :]
    rows, wide = pieces[0].shape
    tile = out.shape[0] // dest.shape[0]
    pairs = wide // (2 * depth)
    first = pl.program_id(0) == 0
    copies = [pltpu.make_async_copy(p, held.at[j], sems.at[j]) for j, p in enumerate(pieces)]

    @pl.when(first)
    def _():
        for copy in copies:
            copy.start()

    for half in range(2):
        total = None
        for j in range(count // 2):
            m = half * (count // 2) + j
            pl.when(first)(copies[m].wait)
            for i in range(pairs):
                for other in range(2):
                    at = pl.multiple_of((2 * i + (side[0] + other) % 2) * depth, depth)
                    term = jnp.dot(
                        held[m, :, pl.ds(at, depth)],
                        panels[other][j * pairs + i],
                        preferred_element_type=jnp.float32,
                    )
                    total = term if total is None else total + term
        total = total.astype(jnp.bfloat16)
        for m in range(rows // tile):
            at = pl.multiple_of(dest[half * rows // tile + m] * tile, tile)
            out[pl.ds(at, tile)] = total[m * tile : (m + 1) * tile]


def project_call(side, dest, here, there, panels, cols, depth):
    rows, wide = here[0].shape
    tile = min(256, cols)
    pieces = list(here) + list(there)
    held = len(here) * wide // 2 // depth
    return pl.pallas_call(
        functools.partial(project_kernel, len(pieces), depth),
        grid_spec=pltpu.PrefetchScalarGridSpec(
            num_scalar_prefetch=2,
            grid=(cols // tile,),
            in_specs=[pl.BlockSpec(memory_space=pl.ANY) for _ in pieces]
            + [
                pl.BlockSpec((held, depth, tile), lambda n, s, d, row=row, at=at // tile: (0, row, at + n))
                for _, row, at in panels
            ],
            out_specs=pl.BlockSpec((2 * rows, tile), lambda n, s, d: (0, n)),
            scratch_shapes=[
                pltpu.VMEM((len(pieces), rows, wide), jnp.bfloat16),
                pltpu.SemaphoreType.DMA((len(pieces),)),
            ],
        ),
        out_shape=jax.ShapeDtypeStruct((2 * rows, cols), jnp.bfloat16),
        compiler_params=pltpu.CompilerParams(vmem_limit_bytes=56 * MIB),
        cost_estimate=LIGHT,
        name="project",
    )(side, dest, *pieces, *(p for p, _, _ in panels))


def stack_kernel(*refs):
    out = refs[-1]
    rows = refs[0].shape[0]
    for m, piece in enumerate(refs[:-1]):
        out[m * rows : (m + 1) * rows] = piece[...]


def stack_call(pieces):
    rows, cols = pieces[0].shape
    tile = min(256, cols)
    return pl.pallas_call(
        stack_kernel,
        grid=(cols // tile,),
        in_specs=[pl.BlockSpec((rows, tile), lambda n: (0, n)) for _ in pieces],
        out_specs=pl.BlockSpec((len(pieces) * rows, tile), lambda n: (0, n)),
        out_shape=jax.ShapeDtypeStruct((len(pieces) * rows, cols), pieces[0].dtype),
        cost_estimate=LIGHT,
        name="stack",
    )(*pieces)


def place_kernel(*refs):
    out, at = refs[-1], 0
    for part in refs[:-1]:
        out[:, at : at + part.shape[2]] = part[0]
        at += part.shape[2]


def place_call(parts, ctx_count):
    count, rows = parts[0].shape[:2]
    wide = sum(p.shape[2] for p in parts)
    return pl.pallas_call(
        place_kernel,
        grid=(count,),
        in_specs=[pl.BlockSpec((1, rows, p.shape[2]), lambda s: (s, 0, 0)) for p in parts],
        out_specs=pl.BlockSpec(
            (rows, wide), lambda s: (0, (s % ctx_count) * (count // ctx_count) + s // ctx_count)
        ),
        out_shape=jax.ShapeDtypeStruct((rows, count * wide), parts[0].dtype),
        compiler_params=pltpu.CompilerParams(vmem_limit_bytes=16 * MIB),
        cost_estimate=LIGHT,
        name="place",
    )(*parts)


def after(value, *others):
    return lax.optimization_barrier((value,) + others)[0]


def on_device(loaded, route, doc_ids, short_filter, medium_filter, out_weight):
    tok_rows, wide = loaded.shape
    channels = wide // 3
    count = lax.axis_size(FSDP)
    ctx_count = lax.axis_size(CTX)
    blk = tok_rows // count
    short_len = short_filter.shape[0]
    depth = short_len - 1
    medium_len = medium_filter.shape[0]
    group_size = wide // short_filter.shape[1]
    length = doc_ids.shape[1]
    cols = channels // CHUNKS
    ctx_at = lax.axis_index(CTX)
    f_at = lax.axis_index(FSDP)
    x_at = lax.axis_index("fx")

    shift = []
    for f in range(count):
        for c in range(ctx_count):
            if f + 1 < count:
                shift.append((f * ctx_count + c, (f + 1) * ctx_count + c))
            elif c + 1 < ctx_count:
                shift.append((f * ctx_count + c, c + 1))

    live, flying = {}, {}

    seqs = jnp.arange(count, dtype=jnp.int32)
    order = jnp.sum(jnp.where(route[0][None, :] == seqs[:, None], seqs[None, :], 0), axis=1)
    blocks = loaded.reshape(count, blk, wide)
    tails = []
    for i in range(2):
        parts = [
            blocks[:, blk - depth :, at : at + channels // 2]
            for at in range(i * channels // 2, wide, channels)
        ]
        tails.append(jnp.concatenate(parts, axis=2).reshape(count * depth, wide // 2))
    direct = lax.ppermute(tails[0], EVERY, shift).reshape(count, depth, wide // 2)

    own_ids = jnp.concatenate([jnp.full((depth,), -1, jnp.int32), doc_ids[0]])
    own_ids = lax.dynamic_slice_in_dim(own_ids, ctx_at * tok_rows, depth + tok_rows, 0)
    near = jnp.stack([own_ids[f * blk : (f + 1) * blk + depth] for f in range(count)])
    order_prev = lax.ppermute(after(order, tails[0]), EVERY, shift)
    near = after(near, tails[0])
    near = lax.all_to_all(near, FSDP, split_axis=0, concat_axis=0, tiled=True)


    taps_full = jnp.repeat(short_filter, group_size, axis=1)

    half = out_weight.shape[1] // 2
    keep = lax.dynamic_slice_in_dim(after(out_weight, tails[0]), x_at * half, half, 1)
    give = lax.dynamic_slice_in_dim(out_weight, (1 - x_at) * half, half, 1)

    reach = ROWS - medium_len
    medium_rows = jnp.pad(
        medium_filter.astype(jnp.float32)[::-1].T, ((0, 0), (reach + 1, ROWS - 1))
    )
    own = jnp.concatenate([jnp.full((ROWS,), -1, jnp.int32), doc_ids[0]])
    own = lax.dynamic_slice_in_dim(own, ctx_at * tok_rows, ROWS + tok_rows, 0)
    same = jnp.stack(
        [
            own[ROWS + a : 2 * ROWS + a][:, None] == own[a : 2 * ROWS + a][None, :]
            for a in range(0, tok_rows, ROWS)
        ]
    ).astype(jnp.bfloat16)

    next_ctx = [(c, c + 1) for c in range(ctx_count - 1)]

    def exchange(sent):
        routed = lax.all_to_all(sent, FSDP, split_axis=0, concat_axis=0, tiled=True)
        return routed.reshape(tok_rows, 2 * cols)

    def cut(kind, first, wide):
        at = half // QUARTERS * first
        return live[kind][:, at : at + half // QUARTERS * wide]

    def fence(step):
        for key in [k for k, (due, _) in flying.items() if due <= step]:
            live[key] = flying.pop(key)[1]
        if step > FENCED:
            return
        keys = list(live)
        for key, value in zip(keys, lax.optimization_barrier([live[k] for k in keys])):
            live[key] = value

    def start_panels(step):
        for kind, first, wide, begin, due in PANEL_STEPS:
            if begin == step:
                kinds = ("keep", "got") if kind == "both" else (kind,)
                part = jnp.concatenate([cut(k, first, wide) for k in kinds], axis=0)
                flying[kind, first, wide] = (due, lax.all_gather(part[None], "fh", axis=0, tiled=True))

    live["keep"] = keep
    start_panels(0)
    direct, near, order_prev = lax.optimization_barrier((direct, near, order_prev))
    mask = jnp.stack(
        [near[:, depth - i : depth - i + blk] == near[:, depth:] for i in range(short_len)], axis=-1
    ).astype(jnp.float32)
    live["give"] = give
    rest = lax.ppermute(after(tails[1], tails[0]), EVERY, shift).reshape(count, depth, wide // 2)
    flying["halo"] = (2, rest)
    live["sent", 0] = short_call(order, order_prev, blocks, direct, taps_full, mask, 0)
    live["mask"] = mask
    live["prior"] = order_prev
    live["medium"] = medium_rows
    live["same"] = same
    place = jnp.arange(2 * ctx_count, dtype=jnp.int32)
    dest = x_at * ctx_count + ctx_at
    dest = dest ^ ((place & 4) // 4 + (place & 2) * 2 + (place & 1) * 2)
    side = x_at.reshape(1)
    unit = half // QUARTERS

    def project(low, high, first, wide, sums=None):
        held = {**live, **{k: v for k, (_, v) in flying.items()}}
        panels = []
        for other, kind in enumerate(("keep", "got")):
            for key in [k for k in held if isinstance(k, tuple) and len(k) == 3 and k[0] in (kind, "both")]:
                if key[1] <= first < key[1] + key[2]:
                    row = other if key[0] == "both" else 0
                    panels.append((held[key], row, (first - key[1]) * unit))
        here, there = ([held[k, j] for j in range(low, high)] for k in ("here", "there"))
        depth = out_weight.shape[0]
        return project_call(side, dest, here, there, panels, unit * wide, depth)


    def stack_steps(step, j):
        if FENCED <= step and j < CHUNKS - 1:
            live["gated", j] = after(live["gated", j], live["by_x", CHUNKS - 1])
        here = stack_call([live.pop((k, j)) for k in ("gated", "by_y", "by_x", "by_both")])
        flying["here", j] = (step, here)
        flying["there", j] = (step + 1, lax.ppermute(here, "core", SWAP))

    last = CHUNKS + 4
    for step in range(1, last + 1):
        fence(step)
        start_panels(step)
        if step == 1:
            flying["got"] = (2, lax.ppermute(live.pop("give"), "fx", SWAP))
        if step <= CHUNKS:
            flying["routed", step - 1] = (step, exchange(live.pop(("sent", step - 1))))
        for j in [j for j in range(CHUNKS) if step == j + 4 - (j in NEAR_EARLY)]:
            if j < VIA_X:
                flying["by_both", j] = (step, lax.ppermute(live["by_x", j], "y", SWAP))
        j = step - 3
        if 0 <= j < CHUNKS and j not in NEAR_EARLY:
            live["gated", j] = after(live["gated", j], live["by_both", j - 1])
            flying["by_x", j] = (step, lax.ppermute(live["gated", j], "fx", SWAP))
            flying["by_y", j] = (step, lax.ppermute(live["gated", j], "y", SWAP))
            across = [(0, 3), (1, 2), (2, 1), (3, 0)]
            flying["by_both", j] = (step, lax.ppermute(live["gated", j], ("fx", "y"), across))
        j = step - 2
        if 0 <= j < CHUNKS:
            routed = live.pop(("routed", j))
            before = lax.ppermute(routed[tok_rows - ROWS :, cols:], CTX, next_ctx)
            gated = medium_call(routed, before, live["medium"], live["same"], j, group_size)
            flying["gated", j] = (step, gated)
            if j in NEAR_EARLY:
                flying["by_x", j] = (step, lax.ppermute(gated, "fx", SWAP))
                flying["by_y", j] = (step, lax.ppermute(gated, "y", SWAP))
        for j in [j for j in range(CHUNKS) if step == (4, 7, 7, 8)[j]]:
            stack_steps(step, j)
        if step < CHUNKS:
            halo = direct if step < CHUNKS // 2 else live["halo"]
            sent = short_call(order, live["prior"], blocks, halo, taps_full, live["mask"], step)
            flying["sent", step] = (step, sent)
    fence(last + 1)
    live.update({k: v for k, (_, v) in flying.items()})

    parts, product = [], None
    for n, (first, wide) in enumerate(PROJECTS):
        if n > 0:
            live["here", 0] = after(live["here", 0], product)
        product = project(0, CHUNKS, first, wide)
        given = product.reshape(-1, tok_rows, product.shape[1])
        if parts:
            given = after(given, parts[-1])
        parts.append(lax.all_to_all(given, PLANE, split_axis=0, concat_axis=0, tiled=True))
    return place_call(parts, ctx_count)


def solution(mesh):
    count, ctx_count = mesh.devices.shape
    fine = Mesh(mesh.devices.reshape(count // 2, 2, ctx_count // 2, 2), EVERY)
    placed = (
        P(EVERY, None),
        P(EVERY, None),
        P(FSDP, None),
        P(),
        P(),
        P(FSDP, CTX),
    )
    return jax.shard_map(
        on_device, mesh=fine, in_specs=placed, out_specs=P(EVERY, None), check_vma=False
    )
```
